32 devices in a mesh: cols: 8 (over y, x, core), gpt: 4 (over z).
Axes of the slice: x: 2, y: 2, z: 4, core: 2. Of those that a mesh axis runs over, the one named last changes fastest.
Arguments:
- starting_warmth: float32 [64, 16384], P('gpt', 'cols'), may hold values from 0.5 to 1.5
- starting_moisture: float32 [64, 16384], P('gpt', 'cols'), may hold values from 0.2 to 2
- spreading_coeffs: float32 [64, 16384], P('gpt', 'cols'), may hold values from 0.05 to 0.3
- neighbour_shifts: int32 [3, 16384], P(None, 'cols'), may hold values from -4 to 4
- daylight_mask: int32 [2048], P('cols'), may hold values from 0 to 1, as said below
- sun_angle_factors: float32 [16384], P('cols'), may hold values from 0.05 to 1
- attenuation_coeffs: float32 [224, 64], P('gpt'), may hold values from 0.002 to 0.5
- thermal_emission_weights: float32 [224], P('gpt'), may hold values from 0.01 to 0.1
- sunlight_arriving: float32 [224], P('gpt'), may hold values from 0.02 to 0.2
Outputs:
- new_temperature: float32 [64, 16384], P('gpt', 'cols')
- new_vapour: float32 [64, 16384], P('gpt', 'cols')
The draws below stay inside these ranges and needn't reach their ends.
Inputs may be any that keep to these rules, and one draw needn't show every extreme that they name: `daylight_mask`: blocks are numbered by cols index, 256 to an index. The sunlit blocks of a cols index and those of the index half the cols axis away number exactly 256 together.
All inputs are finite; a program needn't handle non-finite values.
Results may differ from the reference program's by a relative error of at most 0.0001.
Values sent between devices are 32-bit elements; how exact they have to be, the bound alone decides.
No kernel may reach another device: no remote copies, remote signals or barrier semaphores. Data moves between devices by JAX's collectives and lax.ppermute only.
A program may use at most 64 MiB of HBM per device.

```python
import math
import jax
import jax.numpy as jnp
from jax import lax

GPTS = 224
NB = 256
BC = 8
KSUB = 4
HALO = 4
VERTICAL_SIZE = 64
GRID_COLUMNS_ALL = 16384
BLOCKS = 2048


def draw_daylight_mask(key, part):
    key = jax.random.fold_in(key, 7)
    key_start, key_deficit, key_order = jax.random.split(key, 3)
    col_count = BLOCKS // NB
    half_cols = col_count // 2
    start_col = jax.random.randint(key_start, (), 0, col_count)
    positions = jnp.arange(half_cols, dtype=jnp.int32)
    daylit = (positions - start_col) % col_count < half_cols
    deficit = jax.random.randint(key_deficit, (half_cols,), 0, NB // 4 + 1)
    lower_counts = jnp.where(daylit, NB - deficit, deficit)
    counts = jnp.concatenate([lower_counts, NB - lower_counts])
    order_keys = jax.random.split(key_order, col_count)
    ranks = jax.vmap(lambda one_key: jax.random.permutation(one_key, NB))(order_keys)
    return (ranks < counts[:, None]).astype(jnp.int32).reshape(col_count * NB)


def plant(entries, key, least, largest):
    spot = [jax.random.randint(jax.random.fold_in(key, axis), (), 0, length) for axis, length in enumerate(entries.shape)]
    widest = entries.shape.index(max(entries.shape))
    beside = spot[:widest] + [(spot[widest] + 1) % entries.shape[widest]] + spot[widest + 1:]
    return entries.at[tuple(spot)].set(least).at[tuple(beside)].set(largest)


def level_of(key, shape, shards, least, top_value):
    gain, own = 1.0, jax.random.fold_in(key, 6)
    for position, parts in shards:
        draws = jnp.exp(jax.random.uniform(jax.random.fold_in(own, position), (parts,), jnp.float32, least / len(shards), top_value / len(shards)))
        gain = gain * jnp.repeat(draws, shape[position] // parts).reshape([-1 if axis == position else 1 for axis in range(len(shape))])
    return gain


def setup_inputs(seed: int = 0) -> dict:
    key_of = jax.random.split(jax.random.key(seed), 10)
    starting_warmth = jnp.clip(0.5 + 1.0 * jax.random.uniform(key_of[0], (VERTICAL_SIZE, GRID_COLUMNS_ALL), jnp.float32) ** level_of(key_of[0], (VERTICAL_SIZE, GRID_COLUMNS_ALL), ((0, 4), (1, 8)), -0.2, 0.2), 0.5, 1.5)
    starting_moisture = jnp.clip(jnp.exp(math.log(2.0) - 2.3025851 * jax.random.uniform(key_of[1], (VERTICAL_SIZE, GRID_COLUMNS_ALL), jnp.float32) ** level_of(key_of[1], (VERTICAL_SIZE, GRID_COLUMNS_ALL), ((0, 4), (1, 8)), -0.2, 0.2)), 0.2, 2.0)
    spreading_coeffs = jnp.clip(0.05 + 0.25 * jax.random.uniform(key_of[2], (VERTICAL_SIZE, GRID_COLUMNS_ALL), jnp.float32) ** level_of(key_of[2], (VERTICAL_SIZE, GRID_COLUMNS_ALL), ((0, 4), (1, 8)), -0.2, 0.2), 0.05, 0.3)
    neighbour_shifts = plant(jax.random.randint(key_of[3], (3, GRID_COLUMNS_ALL), 0 - HALO, HALO + 1), jax.random.fold_in(key_of[3], 1), 0 - HALO, HALO).astype(jnp.int32)
    daylight_mask = draw_daylight_mask(jax.random.fold_in(key_of[9], 71), 0)
    sun_angle_factors = jnp.clip(0.05 + 0.95 * jax.random.uniform(key_of[5], (GRID_COLUMNS_ALL,), jnp.float32) ** level_of(key_of[5], (GRID_COLUMNS_ALL,), ((0, 8),), -0.2, 0.2), 0.05, 1.0)
    attenuation_coeffs = jnp.clip(jnp.exp(math.log(0.5) - 5.521461 * jax.random.uniform(key_of[6], (GPTS, VERTICAL_SIZE), jnp.float32) ** level_of(key_of[6], (GPTS, VERTICAL_SIZE), ((0, 4),), -0.2, 0.2)), 0.002, 0.5)
    thermal_emission_weights = jnp.clip(jnp.exp(math.log(0.1) - 2.3025851 * jax.random.uniform(key_of[7], (GPTS,), jnp.float32) ** level_of(key_of[7], (GPTS,), ((0, 4),), -0.2, 0.2)), 0.01, 0.1)
    sunlight_arriving = jnp.clip(jnp.exp(math.log(0.2) - 2.3025851 * jax.random.uniform(key_of[8], (GPTS,), jnp.float32) ** level_of(key_of[8], (GPTS,), ((0, 4),), -0.2, 0.2)), 0.02, 0.2)
    return dict(starting_warmth=starting_warmth, starting_moisture=starting_moisture, spreading_coeffs=spreading_coeffs, neighbour_shifts=neighbour_shifts, daylight_mask=daylight_mask, sun_angle_factors=sun_angle_factors, attenuation_coeffs=attenuation_coeffs, thermal_emission_weights=thermal_emission_weights, sunlight_arriving=sunlight_arriving)


surface_reflectance = 0.3


def evaluate_shortwave(warmth_strata, moisture_strata, sun_elevation_factor, attenuation_coeffs, thermal_emission_weights, sunlight_arriving):
    def level_pass(flux_now, given_tensors):
        extinction_thickness, stratum_warmth, stratum_moisture = given_tensors
        transmit = jnp.exp(-extinction_thickness[:, None] * stratum_moisture[None, :])
        emission_contribution = thermal_emission_weights[:, None] * stratum_warmth[None, :]
        updated = transmit * flux_now + (1.0 - transmit) * emission_contribution
        return updated, jnp.sum(flux_now - updated, axis=0)

    given_tensors = (attenuation_coeffs.T, warmth_strata, moisture_strata)
    bottom_stratum, heat_down = lax.scan(level_pass, sunlight_arriving[:, None] * sun_elevation_factor[None, :], given_tensors)
    rising_beginning = surface_reflectance * bottom_stratum + thermal_emission_weights[:, None] * warmth_strata[-1][None, :]
    _, heat_up = lax.scan(level_pass, rising_beginning, given_tensors, reverse=True)
    return heat_down + heat_up


def reference(starting_warmth, starting_moisture, spreading_coeffs, neighbour_shifts, daylight_mask, sun_angle_factors, attenuation_coeffs, thermal_emission_weights, sunlight_arriving):
    prognostic_tensors = jnp.stack([starting_warmth, starting_moisture])
    neighbours_at = (jnp.arange(GRID_COLUMNS_ALL, dtype=jnp.int32)[None, :] + neighbour_shifts) % GRID_COLUMNS_ALL
    for substep_index in range(KSUB):
        change = jnp.zeros_like(prognostic_tensors)
        for neighbour in range(3):
            change = change + (jnp.take(prognostic_tensors, neighbours_at[neighbour], axis=2) - prognostic_tensors)
        prognostic_tensors = prognostic_tensors + spreading_coeffs[None] * change
    piece_width = math.gcd(GRID_COLUMNS_ALL, 4096)
    piece_amount = GRID_COLUMNS_ALL // piece_width
    warmth_pieces = starting_warmth.reshape(VERTICAL_SIZE, piece_amount, piece_width).transpose(1, 0, 2)
    moisture_pieces = starting_moisture.reshape(VERTICAL_SIZE, piece_amount, piece_width).transpose(1, 0, 2)
    sun_angle_pieces = sun_angle_factors.reshape(piece_amount, piece_width)

    def single_piece(pieces):
        return evaluate_shortwave(pieces[0], pieces[1], pieces[2], attenuation_coeffs, thermal_emission_weights, sunlight_arriving)

    warming_pieces = lax.map(single_piece, (warmth_pieces, moisture_pieces, sun_angle_pieces))
    heating = warming_pieces.transpose(1, 0, 2).reshape(VERTICAL_SIZE, GRID_COLUMNS_ALL)
    lit_columns = jnp.repeat(daylight_mask, BC).astype(jnp.float32)
    return prognostic_tensors[0] + heating * lit_columns[None, :], prognostic_tensors[1]
```

```python
import functools
import math

import jax
import jax.numpy as jnp
from jax import lax
from jax.experimental import pallas as pl
from jax.experimental.pallas import tpu as pltpu
from jax.sharding import PartitionSpec as P

KSUB = 4
HALO = 4
SURFACE = 0.3
LOG2E = math.log2(math.e)
LANES = 128
SUB = 8
GROUP = 4
VMEM = pl.BlockSpec(memory_space=pltpu.VMEM)
F32 = jnp.float32


def params():
    return pltpu.CompilerParams(vmem_limit_bytes=50 * 1024 * 1024)


def shape(*dims):
    return jax.ShapeDtypeStruct(dims, F32)


def pack_kernel(parts, warm, moist, coef, shifts, att, emis, sun_in, *outs):
    sends, head, tail = outs[:parts], outs[parts], outs[parts + 1]
    me = lax.axis_index("gpt")
    rows, cols = warm.shape
    chunk = cols // parts
    points, levels = att.shape
    blocks = points // SUB
    lane = lax.broadcasted_iota(jnp.int32, (SUB, points), 1)
    row = lax.broadcasted_iota(jnp.int32, (SUB, points), 0)
    spot = lax.broadcasted_iota(jnp.int32, (SUB, chunk - blocks * levels), 1)
    extra = jnp.zeros(spot.shape, F32)
    for b in range(blocks):
        hit = lane == row + b * SUB
        w = jnp.sum(jnp.where(hit, emis[...], 0.0), axis=1, keepdims=True)
        s = jnp.sum(jnp.where(hit, sun_in[...], 0.0), axis=1, keepdims=True)
        extra = jnp.where(spot == b, w, extra)
        extra = jnp.where(spot == blocks + b, s, extra)
    for k in range(parts):
        owner = lax.rem(me + k, parts)
        here = pl.ds(pl.multiple_of(owner * chunk, chunk), chunk)
        sends[k][0:rows, :] = warm[:, here]
        sends[k][rows : 2 * rows, :] = moist[:, here]
        for b in range(blocks):
            sends[k][2 * rows :, b * levels : (b + 1) * levels] = att[b * SUB : (b + 1) * SUB, :]
        sends[k][2 * rows :, blocks * levels :] = extra
    for out, at in ((head, 0), (tail, cols - LANES)):
        out[0:rows, :] = warm[:, at : at + LANES]
        out[rows : 2 * rows, :] = moist[:, at : at + LANES]
        out[2 * rows : 3 * rows, :] = coef[:, at : at + LANES]
        out[3 * rows :, :] = jnp.zeros((SUB, LANES), F32)
        out[3 * rows : 3 * rows + 3, :] = shifts[:, at : at + LANES].astype(F32)


def diffuse_kernel(warm, moist, coef, shifts, left, right, mask, out_warm, out_moist, out_lit, field, rate, weight):
    rows, cols = warm.shape
    wide = cols + 2 * LANES
    inner = pl.ds(LANES, cols)
    field[0:rows, inner] = warm[...]
    field[rows:, inner] = moist[...]
    rate[:, inner] = coef[...]
    for got, at in ((left, 0), (right, cols + LANES)):
        there = pl.ds(at, LANES)
        field[:, there] = got[0 : 2 * rows, :]
        rate[:, there] = got[2 * rows : 3 * rows, :]
    shift = jnp.concatenate(
        [left[3 * rows : 3 * rows + 3, :], shifts[...].astype(F32), right[3 * rows : 3 * rows + 3, :]], axis=1
    )
    for o in range(-HALO, HALO + 1):
        hits = jnp.sum((shift == float(o)).astype(F32), axis=0, keepdims=True)
        if o == 0:
            hits = hits - 3.0
        weight[o + HALO] = jnp.broadcast_to(hits, (SUB, wide))
    for _ in range(KSUB):
        for r in range(0, 2 * rows, SUB):
            x = field[r : r + SUB, :]
            total = weight[HALO] * x
            for o in range(1, HALO + 1):
                total = total + weight[HALO + o] * pltpu.roll(x, wide - o, 1)
                total = total + weight[HALO - o] * pltpu.roll(x, o, 1)
            field[r : r + SUB, :] = x + rate[r % rows : r % rows + SUB, :] * total
    out_warm[...] = field[0:rows, inner]
    out_moist[...] = field[rows:, inner]
    count = mask.shape[1]
    each = cols // count
    block = lax.broadcasted_iota(jnp.int32, (count, cols), 0)
    column = lax.broadcasted_iota(jnp.int32, (count, cols), 1)
    spread = ((column >= block * each) & (column < (block + 1) * each)).astype(jnp.bfloat16)
    bits = jnp.broadcast_to(mask[...].astype(F32), (SUB, count)).astype(jnp.bfloat16)
    out_lit[...] = jnp.dot(bits, spread, preferred_element_type=F32)


def radiate_kernel(parts, *refs):
    got = refs[:parts]
    sun = refs[parts]
    sends = refs[parts + 1 : 2 * parts + 1]
    mb, db, ab, ws, tr, acc, heat, temp, moist = refs[2 * parts + 1 :]
    me = lax.axis_index("gpt")
    chunk = got[0].shape[1]
    rows = sends[0].shape[0]
    levels = rows * parts
    blocks = ab.shape[0] // parts
    for k in range(parts):
        source = lax.rem(me + parts - k, parts)
        here = pl.ds(pl.multiple_of(source * rows, rows), rows)
        temp[here, :] = got[k][0:rows, :]
        moist[here, :] = got[k][rows : 2 * rows, :] * (-LOG2E)
        for b in range(blocks):
            tile = got[k][2 * rows :, b * levels : (b + 1) * levels]
            for l in range(levels):
                ab[k * blocks + b, l] = jnp.broadcast_to(tile[:, l : l + 1], (SUB, LANES))
            base = blocks * levels
            w = got[k][2 * rows :, base + b : base + b + 1]
            s = got[k][2 * rows :, base + blocks + b : base + blocks + b + 1]
            ws[k * blocks + b, 0] = jnp.broadcast_to(w, (SUB, LANES))
            ws[k * blocks + b, 1] = jnp.broadcast_to(s / w, (SUB, LANES))

    zero = jnp.zeros((SUB, chunk), F32)
    db[0] = zero
    db[levels] = zero
    for l in range(levels):
        mb[l] = jnp.broadcast_to(moist[l : l + 1, :], (SUB, chunk))
        if l > 0:
            db[l] = jnp.broadcast_to(temp[l - 1 : l, :] - temp[l : l + 1, :], (SUB, chunk))
    top = jnp.broadcast_to(temp[0:1, :], (SUB, chunk))
    bottom = jnp.broadcast_to(temp[levels - 1 : levels, :], (SUB, chunk))

    @pl.loop(0, levels + 1)
    def _(l):
        acc[l] = zero

    mine = pl.ds(pl.multiple_of(me * chunk, chunk), chunk)
    angle = jnp.broadcast_to(sun[:, mine], (SUB, chunk))
    tiles = chunk // LANES

    def cut(x, t):
        return x[:, t * LANES : (t + 1) * LANES]

    @pl.loop(0, parts * blocks // GROUP)
    def _(group):
        first = group * GROUP
        w = [ws[first + j, 0] for j in range(GROUP)]

        def add_up(l, state, sign):
            for t in range(tiles):
                total = w[0] * state[t]
                for j in range(1, GROUP):
                    total = total + w[j] * state[j * tiles + t]
                here = pl.ds(t * LANES, LANES)
                acc[l, :, here] = acc[l, :, here] + total if sign > 0 else acc[l, :, here] - total

        def descend(l, state):
            add_up(l, state, 1)
            fresh = []
            for j in range(GROUP):
                a = ab[first + j, l]
                for t in range(tiles):
                    here = pl.ds(t * LANES, LANES)
                    transmit = jnp.exp2(a * mb[l, :, here])
                    tr[l, j, :, here] = transmit
                    fresh.append(transmit * state[j * tiles + t] + db[l + 1, :, here])
            return tuple(fresh)

        def ascend(i, state):
            l = levels - 1 - i
            fresh = []
            for j in range(GROUP):
                for t in range(tiles):
                    here = pl.ds(t * LANES, LANES)
                    fresh.append(tr[l, j, :, here] * state[j * tiles + t] - db[l, :, here])
            add_up(l, fresh, -1)
            return tuple(fresh)

        state = tuple(
            ws[first + j, 1] * cut(angle, t) - cut(top, t) for j in range(GROUP) for t in range(tiles)
        )
        state = lax.fori_loop(0, levels, descend, state, unroll=4)
        add_up(levels, state, 1)
        state = tuple(
            SURFACE * (state[j * tiles + t] + cut(bottom, t)) for j in range(GROUP) for t in range(tiles)
        )
        add_up(levels, state, -1)
        lax.fori_loop(0, levels, ascend, state, unroll=4)

    weight = jnp.zeros((SUB, LANES), F32)
    for b in range(parts * blocks):
        weight = weight + ws[b, 0]
    for t in range(tiles):
        here = pl.ds(t * LANES, LANES)
        above = acc[0, :, here]
        for l in range(levels):
            below = acc[l + 1, :, here] - weight * db[l + 1, :, here]
            heat[l : l + 1, here] = jnp.sum(above - below, axis=0, keepdims=True)
            above = below
    for k in range(parts):
        owner = lax.rem(me + k, parts)
        sends[k][...] = heat[pl.ds(pl.multiple_of(owner * rows, rows), rows), :]


def add_kernel(parts, warm, lit, *refs):
    got, out = refs[:parts], refs[parts]
    me = lax.axis_index("gpt")
    chunk = got[0].shape[1]
    rows = warm.shape[0]
    for k in range(parts):
        source = lax.rem(me + parts - k, parts)
        here = pl.ds(pl.multiple_of(source * chunk, chunk), chunk)
        for r in range(0, rows, SUB):
            out[r : r + SUB, here] = warm[r : r + SUB, here] + got[k][r : r + SUB, :] * lit[:, here]


def local(parts, ring, warm, moist, coef, shifts, mask, angle, att, emis, sun_in):
    rows, cols = warm.shape
    points, levels = att.shape
    chunk = cols // parts
    total = rows * parts
    blocks = points // SUB

    def around(x, step):
        return lax.ppermute(x, "gpt", [(i, (i + step) % parts) for i in range(parts)])

    packed = pl.pallas_call(
        functools.partial(pack_kernel, parts),
        out_shape=[shape(2 * rows + SUB, chunk)] * parts + [shape(3 * rows + SUB, LANES)] * 2,
        in_specs=[VMEM] * 7,
        out_specs=[VMEM] * (parts + 2),
        compiler_params=params(),
        name="pack",
    )(warm, moist, coef, shifts, att, emis.reshape(1, -1), sun_in.reshape(1, -1))
    sends, head, tail = packed[:parts], packed[parts], packed[parts + 1]
    got = [sends[0]] + [around(sends[k], k) for k in range(1, parts)]
    left = lax.ppermute(tail, "cols", [(i, (i + 1) % ring) for i in range(ring)])
    right = lax.ppermute(head, "cols", [((i + 1) % ring, i) for i in range(ring)])

    new_warm, new_moist, lit = pl.pallas_call(
        diffuse_kernel,
        out_shape=[shape(rows, cols), shape(rows, cols), shape(SUB, cols)],
        in_specs=[VMEM] * 7,
        out_specs=[VMEM] * 3,
        scratch_shapes=[
            pltpu.VMEM((2 * rows, cols + 2 * LANES), F32),
            pltpu.VMEM((rows, cols + 2 * LANES), F32),
            pltpu.VMEM((2 * HALO + 1, SUB, cols + 2 * LANES), F32),
        ],
        compiler_params=params(),
        cost_estimate=pl.CostEstimate(flops=20_000_000, bytes_accessed=1_000_000, transcendentals=0),
        name="diffuse",
    )(warm, moist, coef, shifts, left, right, mask.reshape(1, -1))

    heats = pl.pallas_call(
        functools.partial(radiate_kernel, parts),
        out_shape=[shape(rows, chunk)] * parts,
        in_specs=[VMEM] * (parts + 1),
        out_specs=[VMEM] * parts,
        scratch_shapes=[
            pltpu.VMEM((total, SUB, chunk), F32),
            pltpu.VMEM((total + 1, SUB, chunk), F32),
            pltpu.VMEM((parts * blocks, total, SUB, LANES), F32),
            pltpu.VMEM((parts * blocks, 2, SUB, LANES), F32),
            pltpu.VMEM((total, GROUP, SUB, chunk), F32),
            pltpu.VMEM((total + 1, SUB, chunk), F32),
            pltpu.VMEM((total, chunk), F32),
            pltpu.VMEM((total, chunk), F32),
            pltpu.VMEM((total, chunk), F32),
        ],
        compiler_params=params(),
        cost_estimate=pl.CostEstimate(flops=100_000_000, bytes_accessed=1_000_000, transcendentals=7_000_000),
        name="radiate",
    )(*got, angle.reshape(1, -1))
    back = [heats[0]] + [around(heats[k], k) for k in range(1, parts)]

    new_temp = pl.pallas_call(
        functools.partial(add_kernel, parts),
        out_shape=shape(rows, cols),
        in_specs=[VMEM] * (parts + 2),
        out_specs=VMEM,
        compiler_params=params(),
        name="add_heat",
    )(new_warm, lit, *back)
    return new_temp, new_moist


def solution(mesh):
    return jax.shard_map(
        functools.partial(local, mesh.shape["gpt"], mesh.shape["cols"]),
        mesh=mesh,
        in_specs=(
            P("gpt", "cols"),
            P("gpt", "cols"),
            P("gpt", "cols"),
            P(None, "cols"),
            P("cols"),
            P("cols"),
            P("gpt", None),
            P("gpt"),
            P("gpt"),
        ),
        out_specs=(P("gpt", "cols"), P("gpt", "cols")),
        check_vma=False,
    )
```
